32 devices in a mesh: gx: 8 (over z, x), gy: 4 (over y, core).
Axes of the slice: x: 2, y: 2, z: 4, core: 2. Of those that a mesh axis runs over, the one named last changes fastest.
Arguments:
- distribution_values: float32 [19, 16, 32, 128], P(None, 'gx', 'gy'), may hold values from 0.02 to 0.09
- thermal_field: float32 [16, 32, 128], P('gx', 'gy'), may hold values from -0.5 to 0.5
- site_kind_code: int32 [16, 32, 128], P('gx', 'gy'), may hold values from 0 to 2, as said below
- entry_level_matrix: float32 [19, 128], replicated, may hold values from -16 to 16
- entry_level_offset: float32 [128], replicated, may hold values from -3 to 3
- inner_level_matrix: float32 [128, 128], replicated, may hold values from -0.5 to 0.5
- inner_level_offset: float32 [128], replicated, may hold values from -3 to 3
- exit_level_matrix: float32 [128, 19], replicated, may hold values from -0.125 to 0.125
- exit_level_offset: float32 [19], replicated, may hold values from -0.75 to 0.75
- closing_density_adjoint: float32 [19, 16, 32, 128], P(None, 'gx', 'gy'), may hold values from -6 to 6
- closing_thermal_adjoint: float32 [16, 32, 128], P('gx', 'gy'), may hold values from -6 to 6
Outputs:
- adjoint_populations: float32 [19, 16, 32, 128], P(None, 'gx', 'gy')
- adjoint_temperature: float32 [16, 32, 128], P('gx', 'gy')
- grad_first_weight: float32 [19, 128], replicated
- grad_first_bias: float32 [128], replicated
- grad_second_weight: float32 [128, 128], replicated
- grad_second_bias: float32 [128], replicated
- grad_third_weight: float32 [128, 19], replicated
- grad_third_bias: float32 [19], replicated
The draws below stay inside these ranges and needn't reach their ends.
Inputs may be any that keep to these rules, and one draw needn't show every extreme that they name: `site_kind_code`: 0 marks a fluid cell, 1 a solid cell whose temperature is held, 2 a solid heater cell.
All inputs are finite; a program needn't handle non-finite values.
Results may differ from the reference program's by a relative error of at most 0.0003.
Values sent between devices are 32-bit elements; how exact they have to be, the bound alone decides.
A program may use at most 64 MiB of HBM per device.

```python
import math
import jax
import jax.numpy as jnp
import numpy as np
from jax import lax

Q = 19
HID = 128
STEPS = 2
SITES_ALONG_Z = 128
SITES_ALONG_X = 16
SITES_ALONG_Y = 32


def draw_site_kind_code(key, part):
    picked = jax.random.randint(key, (SITES_ALONG_X, SITES_ALONG_Y, SITES_ALONG_Z), 0, 10)
    return jnp.where(picked == 0, 1, jnp.where(picked == 1, 2, 0)).astype(jnp.int32)


def steps_of(key, dims, split, low, largest):
    loudness = 1.0
    for dim, parts in split:
        steps = jax.random.uniform(jax.random.fold_in(jax.random.fold_in(key, 6), dim), (parts,), jnp.float32, low / len(split), largest / len(split))
        loudness = loudness * jnp.repeat(jnp.exp(steps), dims[dim] // parts).reshape((-1,) + (1,) * (len(dims) - 1 - dim))
    return loudness


def bell_draw(rng, shape, spread, most, pieces=(), held_as=jnp.bfloat16):
    gain = steps_of(rng, shape, pieces, -0.22, 0.18) if pieces else 1.0
    values = jax.random.normal(rng, shape, jnp.float32) * spread * gain
    return jnp.minimum(jnp.maximum(values, -most), most).astype(held_as)


def setup_inputs(seed: int = 0) -> dict:
    key_list = jax.random.split(jax.random.key(seed), 12)
    return {
        "distribution_values": jnp.clip(0.02 + 0.07000000402331352 * jax.random.uniform(key_list[0], (Q, SITES_ALONG_X, SITES_ALONG_Y, SITES_ALONG_Z), jnp.float32) ** steps_of(key_list[0], (Q, SITES_ALONG_X, SITES_ALONG_Y, SITES_ALONG_Z), ((1, 8), (2, 4)), -0.2, 0.2), 0.02, 0.09),
        "thermal_field": jnp.clip(jax.random.uniform(key_list[1], (SITES_ALONG_X, SITES_ALONG_Y, SITES_ALONG_Z), jnp.float32, -0.5, 0.5) * steps_of(key_list[1], (SITES_ALONG_X, SITES_ALONG_Y, SITES_ALONG_Z), ((0, 8), (1, 4)), -0.4, 0.0), -0.5, 0.5),
        "site_kind_code": draw_site_kind_code(jax.random.fold_in(key_list[11], 71), 0),
        "entry_level_matrix": jnp.clip(jax.random.uniform(key_list[3], (Q, HID), jnp.float32, -16.0, 16.0), -16.0, 16.0),
        "entry_level_offset": bell_draw(key_list[4], (HID,), 0.5, 3.0, (), jnp.float32),
        "inner_level_matrix": bell_draw(key_list[5], (HID, HID), HID ** -0.5, 0.5, (), jnp.float32),
        "inner_level_offset": bell_draw(key_list[6], (HID,), 0.5, 3.0, (), jnp.float32),
        "exit_level_matrix": bell_draw(key_list[7], (HID, Q), (16 * HID) ** -0.5, 0.125, (), jnp.float32),
        "exit_level_offset": bell_draw(key_list[8], (Q,), 0.05, 0.75, (), jnp.float32),
        "closing_density_adjoint": bell_draw(key_list[9], (Q, SITES_ALONG_X, SITES_ALONG_Y, SITES_ALONG_Z), 1.0, 6.0, ((1, 8), (2, 4)), jnp.float32),
        "closing_thermal_adjoint": bell_draw(key_list[10], (SITES_ALONG_X, SITES_ALONG_Y, SITES_ALONG_Z), 1.0, 6.0, ((0, 8), (1, 4)), jnp.float32),
    }


VELOCITIES = np.array([[0, 0, 0], [1, 0, 0], [-1, 0, 0], [0, 1, 0], [0, -1, 0], [0, 0, 1], [0, 0, -1], [1, 1, 0], [-1, -1, 0], [1, -1, 0], [-1, 1, 0], [1, 0, 1], [-1, 0, -1], [1, 0, -1], [-1, 0, 1], [0, 1, 1], [0, -1, -1], [0, 1, -1], [0, -1, 1]])
OPPOSITE = np.array([0, 2, 1, 4, 3, 6, 5, 8, 7, 10, 9, 12, 11, 14, 13, 16, 15, 18, 17])
LATTICE_WEIGHTS = np.array([1.0 / 3.0] + [1.0 / 18.0] * 6 + [1.0 / 36.0] * 12)
BUOYANCY = 0.3 * LATTICE_WEIGHTS * VELOCITIES[:, 2]
CONDUCTIVITY = 0.1
HOT_WALL = 0.5
COLD_WALL = -0.5
HEATER = 0.5
PRECISE_MODE = lax.Precision.HIGHEST
CONTRACT = (((0,), (0,)), ((), ()))

def propagation_offset(window, step_z):
    lead = [(0, 0)] * (window.ndim - 1)
    if step_z == 1:
        return jnp.pad(window[..., :-1], lead + [(1, 0)])
    if step_z == -1:
        return jnp.pad(window[..., 1:], lead + [(0, 1)])
    return window

def boundary(cells):
    depths = jnp.arange(cells)
    masks = []
    for i in range(19):
        step_z = int(VELOCITIES[i, 2])
        if step_z == 1:
            masks.append(depths == 0)
        elif step_z == -1:
            masks.append(depths == cells - 1)
        else:
            masks.append(depths < 0)
    return jnp.stack(masks).astype(jnp.float32)[:, None, None, :]

def collide(current_fields, current_thermal, site_kind_code, learned_coefficients):
    entry_level_matrix, entry_level_offset, inner_level_matrix, inner_level_offset, exit_level_matrix, exit_level_offset = learned_coefficients
    flattened = current_fields.reshape(19, -1)
    hidden_one = jnp.tanh(lax.dot_general(entry_level_matrix, flattened, CONTRACT, precision=PRECISE_MODE) + entry_level_offset[:, None])
    hidden_two = jnp.tanh(lax.dot_general(inner_level_matrix, hidden_one, CONTRACT, precision=PRECISE_MODE) + inner_level_offset[:, None])
    output = lax.dot_general(exit_level_matrix, hidden_two, CONTRACT, precision=PRECISE_MODE) + exit_level_offset[:, None]
    lifting = jnp.asarray(BUOYANCY, jnp.float32).reshape((19,) + (1,) * current_thermal.ndim)
    relaxed = current_fields + output.reshape(current_fields.shape) + lifting * current_thermal[None]
    bounced = current_fields[OPPOSITE]
    return jnp.where(site_kind_code[None] == 0, relaxed, bounced)

def motion_of(current_fields):
    lookup_table = jnp.asarray(VELOCITIES.T, jnp.float32)
    return jnp.tensordot(lookup_table, current_fields, axes=1, precision=PRECISE_MODE)

def depth_pad(heat_rim):
    span_along_x, span_along_y, discarded_outcome = heat_rim.shape
    bottom = jnp.full((span_along_x, span_along_y, 1), HOT_WALL, jnp.float32)
    upper = jnp.full((span_along_x, span_along_y, 1), COLD_WALL, jnp.float32)
    return jnp.concatenate([bottom, heat_rim, upper], axis=2)

def advance_temp(padded, current_thermal, motion, site_kind_code):
    span_along_x, span_along_y, span_along_z = current_thermal.shape
    summed = (1.0 - 6.0 * CONDUCTIVITY) * current_thermal
    for a in range(3):
        for s in (1, -1):
            anchor = [1, 1, 1]
            anchor[a] += s
            nearby = padded[anchor[0]:anchor[0] + span_along_x, anchor[1]:anchor[1] + span_along_y, anchor[2]:anchor[2] + span_along_z]
            summed = summed + (CONDUCTIVITY - 0.5 * s * motion[a]) * nearby
    return jnp.where(site_kind_code == 0, summed, jnp.where(site_kind_code == 1, current_thermal, HEATER))

def stream_pull(planes, orient):
    span_along_x = planes[0].shape[0] - 2
    span_along_y = planes[0].shape[1] - 2
    pulled = []
    for i in range(19):
        step_x = int(VELOCITIES[i, 0]) * orient
        step_y = int(VELOCITIES[i, 1]) * orient
        step_z = int(VELOCITIES[i, 2]) * orient
        window = planes[i][1 - step_x:1 - step_x + span_along_x, 1 - step_y:1 - step_y + span_along_y, :]
        pulled.append(propagation_offset(window, step_z))
    return jnp.stack(pulled)

def advance(current_fields, current_thermal, site_kind_code, learned_coefficients):

    def one_plane(items):
        return collide(items[0], items[1], items[2], learned_coefficients)
    post_collide = lax.map(jax.checkpoint(one_plane), (jnp.moveaxis(current_fields, 1, 0), current_thermal, site_kind_code))
    post_collide = jnp.moveaxis(post_collide, 0, 1)
    padded = jnp.pad(post_collide, ((0, 0), (1, 1), (1, 1), (0, 0)), mode='wrap')
    read = stream_pull([padded[i] for i in range(19)], 1) + boundary(current_fields.shape[-1]) * post_collide[OPPOSITE]
    heat_rim = jnp.pad(current_thermal, ((1, 1), (1, 1), (0, 0)), mode='wrap')
    heated = advance_temp(depth_pad(heat_rim), current_thermal, motion_of(current_fields), site_kind_code)
    return (read, heated)

def reference(distribution_values, thermal_field, site_kind_code, entry_level_matrix, entry_level_offset, inner_level_matrix, inner_level_offset, exit_level_matrix, exit_level_offset, closing_density_adjoint, closing_thermal_adjoint):

    def primal_pass(current_fields, current_thermal, learned_coefficients):
        for i in range(STEPS):
            current_fields, current_thermal = advance(current_fields, current_thermal, site_kind_code, learned_coefficients)
        return (current_fields, current_thermal)
    learned_coefficients = (entry_level_matrix, entry_level_offset, inner_level_matrix, inner_level_offset, exit_level_matrix, exit_level_offset)
    discarded_outcome, backpropagation_function = jax.vjp(primal_pass, distribution_values, thermal_field, learned_coefficients)
    density_adjoint, thermal_adjoint, adjoint_sequence = backpropagation_function((closing_density_adjoint, closing_thermal_adjoint))
    factor = 1.0 / math.sqrt(SITES_ALONG_X * SITES_ALONG_Y * SITES_ALONG_Z)
    return (density_adjoint, thermal_adjoint, adjoint_sequence[0] * factor, adjoint_sequence[1] * factor, adjoint_sequence[2] * factor, adjoint_sequence[3] * factor, adjoint_sequence[4] * factor, adjoint_sequence[5] * factor)
```

```python
import functools
import math

import jax
import jax.numpy as jnp
import numpy as np
from jax import lax
from jax.experimental import pallas as pl
from jax.experimental.pallas import tpu as pltpu
from jax.sharding import PartitionSpec as P

VELOCITIES = np.array(
    [
        [0, 0, 0],
        [1, 0, 0],
        [-1, 0, 0],
        [0, 1, 0],
        [0, -1, 0],
        [0, 0, 1],
        [0, 0, -1],
        [1, 1, 0],
        [-1, -1, 0],
        [1, -1, 0],
        [-1, 1, 0],
        [1, 0, 1],
        [-1, 0, -1],
        [1, 0, -1],
        [-1, 0, 1],
        [0, 1, 1],
        [0, -1, -1],
        [0, 1, -1],
        [0, -1, 1],
    ]
)
Q = len(VELOCITIES)
OPPOSITE = [0, 2, 1, 4, 3, 6, 5, 8, 7, 10, 9, 12, 11, 14, 13, 16, 15, 18, 17]
LATTICE_WEIGHTS = np.array([1.0 / 3.0] + [1.0 / 18.0] * 6 + [1.0 / 36.0] * 12)
BUOYANCY = [float(v) for v in 0.3 * LATTICE_WEIGHTS * VELOCITIES[:, 2]]
CONDUCTIVITY = 0.1
HOT_WALL = 0.5
COLD_WALL = -0.5
HEATER = 0.5
SIGNS = (1, -1)
CORNERS = [(1, 1), (1, -1), (-1, 1), (-1, -1)]
LANES = 128
ROWS = 32
SLOTS = 6
MESH = pl.DeviceIdType.MESH
BF16 = jnp.bfloat16
F32 = jnp.float32
NN = (((1,), (0,)), ((), ()))
NT = (((1,), (1,)), ((), ()))


def steps_of(orient):
    return [tuple(int(v) * orient for v in VELOCITIES[i]) for i in range(Q)]


def movers(orient, axis, sign):
    return [i for i, step in enumerate(steps_of(orient)) if step[axis] == sign]


def corner_mover(orient, dx, dy):
    return steps_of(orient).index((dx, dy, 0))


def halves(values):
    high = values.astype(BF16)
    return high, (values - high.astype(F32)).astype(BF16)


def dot(a, b, dims):
    return lax.dot_general(a, b, dims, preferred_element_type=F32)


def kernel(
    sizes,
    f0, t0, site, w1, b1, w2, b2, w3, b3, adj2, tadj2,
    adj_out, tadj_out, gw1, gb1, gw2, gb2, gw3, gb3,
    post, f1, t1, adj1, tadj1, net, pcg, pcgf,
    ft, pt, h1, h2, h1c, h2c, d1c, d2c,
    square, m1, m2, m3, r1, r2, r3, col,
    sx, sy, sc, rx, ry, rc, send, recv,
    grads, parts_y, parts_x, total, gsend, grecv,
):
    nx, ny, nz, ngx, ngy, factor = sizes
    cols = nx * ny
    sites = cols * nz
    hid = w2.shape[0]
    chunk = min(4, cols)
    gx, gy = lax.axis_index("gx"), lax.axis_index("gy")

    def device(dx, dy):
        return (lax.rem(gx + dx + ngx, ngx), lax.rem(gy + dy + ngy, ngy))

    barrier = pltpu.get_barrier_semaphore()
    partners = [(d, 0) for d in range(1, ngx)] + [(0, d) for d in range(1, ngy)] + CORNERS
    for dx, dy in partners:
        pl.semaphore_signal(barrier, inc=1, device_id=device(dx, dy), device_id_type=MESH)

    def rows(i, x):
        return pl.ds((i * nx + x) * ny, ny)

    def row(i, x, y):
        return pl.ds((i * nx + x) * ny + y, 1)

    depth = lax.broadcasted_iota(jnp.int32, (ny, nz), 1)
    height = lax.broadcasted_iota(jnp.int32, (ny, nz), 0)

    square[...] = jnp.zeros_like(square)
    square[0:Q, :] = w1[...]
    square[Q : Q + 1, :] = b1[...]
    w1_rows = square[...]
    a, b = halves(jnp.transpose(w1_rows)[:, :ROWS])
    m1[...] = jnp.concatenate([a, a, b], axis=1)
    a, b = halves(w1_rows[:ROWS])
    r1[...] = jnp.concatenate(
        [jnp.concatenate([a, a], axis=1), jnp.concatenate([b, jnp.zeros_like(b)], axis=1)], axis=0
    )
    for matrix, target in ((jnp.transpose(w2[...]), m2), (w2[...], r2)):
        a, b = halves(matrix)
        target[...] = jnp.concatenate(
            [jnp.concatenate([a, a], axis=1), jnp.concatenate([b, jnp.zeros_like(b)], axis=1)],
            axis=0,
        )
    square[...] = jnp.zeros_like(square)
    square[:, 0:Q] = w3[...]
    w3_cols = square[...]
    a, b = halves(jnp.transpose(w3_cols)[:ROWS])
    m3[...] = jnp.concatenate(
        [jnp.concatenate([a, a], axis=1), jnp.concatenate([b, jnp.zeros_like(b)], axis=1)], axis=0
    )
    a, b = halves(w3_cols[:, :ROWS])
    r3[...] = jnp.concatenate([a, a, b], axis=1)
    square[...] = jnp.zeros_like(square)
    square[0:1, :] = b2[...]
    square[1:2, 0:Q] = b3[...]
    col[...] = jnp.transpose(square[...])

    for s in range(2):
        ft[s] = jnp.zeros((ROWS, sites), F32)
        ft[s, Q : Q + 1, :] = jnp.ones((1, sites), F32)
    pt[...] = jnp.zeros_like(pt)

    def to_rows(source, target):
        for c in range(cols):
            target[0:Q, c * nz : (c + 1) * nz] = source[pl.ds(c, Q, stride=cols), :]

    def to_planes(values, first, target):
        for c in range(chunk):
            target[pl.ds(first + c, Q, stride=cols), :] = values[0:Q, c * nz : (c + 1) * nz]

    def chunks():
        for first in range(0, cols, chunk):
            yield first, pl.ds(first * nz, chunk * nz)

    def hidden(s, at):
        a, b = halves(ft[s, :, at])
        one = jnp.tanh(dot(m1[...], jnp.concatenate([a, b, a], axis=0), NN))
        h1[s, :, at] = one
        pair = jnp.concatenate(halves(one), axis=0)
        h1c[s, :, at] = pair
        both = dot(m2[...], pair, NN)
        two = jnp.tanh(both[:hid] + both[hid:] + col[:, 0:1])
        h2[s, :, at] = two
        pair = jnp.concatenate(halves(two), axis=0)
        h2c[s, :, at] = pair
        return pair

    def network_back(s, first, at):
        a, b = halves(pt[s, :, at])
        back = dot(r3[...], jnp.concatenate([a, b, a], axis=0), NN)
        two = h2[s, :, at]
        pair = jnp.concatenate(halves(back * (1.0 - two * two)), axis=0)
        d2c[s, :, at] = pair
        both = dot(r2[...], pair, NN)
        one = h1[s, :, at]
        pair = jnp.concatenate(halves((both[:hid] + both[hid:]) * (1.0 - one * one)), axis=0)
        d1c[s, :, at] = pair
        both = dot(r1[...], pair, NN)
        to_planes(both[:ROWS] + both[ROWS:], first, net)

    def folded(product, n, m):
        return product[:n, :m] + product[:n, m : 2 * m] + product[n : 2 * n, :m]

    at1, at2 = 0, ROWS
    at3 = at2 + hid
    at4 = at3 + 8
    at5 = at4 + ROWS

    def weight_grads(s):
        pairs = dot(jnp.concatenate(halves(ft[s]), axis=0), d1c[s], NT)
        first = folded(pairs, ROWS, hid)
        ones = jnp.ones((16, sites), BF16)
        pairs = dot(jnp.concatenate([h1c[s], ones], axis=0), d2c[s], NT)
        second = folded(pairs, hid, hid)
        second_bias = pairs[2 * hid : 2 * hid + 8, :hid] + pairs[2 * hid : 2 * hid + 8, hid:]
        pairs = dot(jnp.concatenate(halves(pt[s]), axis=0), h2c[s], NT)
        third = folded(pairs, ROWS, hid)
        third_bias = jnp.broadcast_to(jnp.sum(pt[s], axis=1, keepdims=True), (ROWS, LANES))
        for start, value in (
            (at1, first), (at2, second), (at3, second_bias), (at4, third), (at5, third_bias)
        ):
            where = pl.ds(start, value.shape[0])
            if s == 1:
                grads[where, :] = value
            else:
                grads[where, :] = (grads[where, :] + value) * factor

    started = []

    def begin(e, source, orient, extras, corners):
        found = {}
        for k, sign in enumerate(SIGNS):
            slot = 0
            for i in movers(orient, 0, sign) if source is not None else ():
                sx[e, k, slot * ny : (slot + 1) * ny, :] = source[
                    rows(i, nx - 1 if sign == 1 else 0), :
                ]
                slot += 1
            for extra in extras:
                sx[e, k, slot * ny : (slot + 1) * ny, :] = extra(
                    0, sign, nx - 1 if sign == 1 else 0
                )
                slot += 1
            slot = 0
            edge = ny - 1 if sign == 1 else 0
            for i in movers(orient, 1, sign) if source is not None else ():
                for x in range(nx):
                    sy[e, k, slot * nx + x : slot * nx + x + 1, :] = source[row(i, x, edge), :]
                slot += 1
            for extra in extras:
                for x in range(nx):
                    sy[e, k, slot * nx + x : slot * nx + x + 1, :] = extra(1, sign, x)[
                        edge : edge + 1, :
                    ]
                slot += 1
        if corners:
            for k, (dx, dy) in enumerate(CORNERS):
                i = corner_mover(orient, dx, dy)
                sc[e, k, 0:1, :] = source[
                    row(i, nx - 1 if dx == 1 else 0, ny - 1 if dy == 1 else 0), :
                ]

        def copy(src, dst, n, dx, dy):
            found[n] = pltpu.make_async_remote_copy(
                src_ref=src, dst_ref=dst, send_sem=send.at[e, n], recv_sem=recv.at[e, n],
                device_id=device(dx, dy), device_id_type=MESH,
            )
            found[n].start()

        for k, sign in enumerate(SIGNS):
            copy(sx.at[e, k], rx.at[e, k], k, sign, 0)
            copy(sy.at[e, k], ry.at[e, k], 2 + k, 0, sign)
        if corners:
            for k, (dx, dy) in enumerate(CORNERS):
                copy(sc.at[e, k], rc.at[e, k], 4 + k, dx, dy)
        started.extend(found.values())
        return list(found.values())

    def arrive(copies):
        for c in copies:
            c.wait_recv()

    def moved_x(inside, e, slot, x, sign):
        if 0 <= x - sign < nx:
            return inside(x - sign)
        return rx[e, SIGNS.index(sign), slot * ny : (slot + 1) * ny, :]

    def moved_y(plane, edge_row, sign):
        shifted = pltpu.roll(plane, 1 if sign == 1 else ny - 1, 0)
        edge = 0 if sign == 1 else ny - 1
        return jnp.where(height == edge, jnp.broadcast_to(edge_row, shifted.shape), shifted)

    def moved_z(plane, fill, sign):
        shifted = pltpu.roll(plane, 1 if sign == 1 else nz - 1, 1)
        return jnp.where(depth == (0 if sign == 1 else nz - 1), fill, shifted)

    def face_y(e, slot, x, sign):
        at = slot * nx + x
        return ry[e, SIGNS.index(sign), at : at + 1, :]

    def stream(source, e, orient, store):
        for i, (px, py, pz) in enumerate(steps_of(orient)):
            for x in range(nx):
                plane = None
                if px:
                    plane = moved_x(
                        lambda k: source[rows(i, k), :],
                        e, movers(orient, 0, px).index(i), x, px,
                    )
                else:
                    plane = source[rows(i, x), :]
                if py:
                    if 0 <= x - px < nx:
                        edge = face_y(e, movers(orient, 1, py).index(i), x - px, py)
                    else:
                        edge = rc[e, CORNERS.index((px, py)), 0:1, :]
                    plane = moved_y(plane, edge, py)
                if pz:
                    plane = moved_z(plane, source[rows(OPPOSITE[i], x), :], pz)
                store(i, x, plane)

    def motion(fields, x):
        result = []
        for a in range(3):
            value = None
            for i in range(Q):
                if VELOCITIES[i, a] == 0:
                    continue
                term = fields[rows(i, x), :]
                if value is None:
                    value = term if VELOCITIES[i, a] == 1 else -term
                elif VELOCITIES[i, a] == 1:
                    value = value + term
                else:
                    value = value - term
            result.append(value)
        return result

    def heat_near(field, e, slot, x, a, s):
        if a == 0:
            return moved_x(lambda k: field[k], e, slot, x, -s)
        if a == 1:
            return moved_y(field[x], face_y(e, slot, x, -s), -s)
        return moved_z(field[x], COLD_WALL if s == 1 else HOT_WALL, -s)

    def fluid(x):
        return site[x] == 0

    def liquid(tadj, x):
        return jnp.where(fluid(x), tadj[x], 0.0)

    def flux(fields, tadj, x, a, s):
        return (CONDUCTIVITY - 0.5 * s * motion(fields, x)[a]) * liquid(tadj, x)

    to_rows(f0, ft.at[0])
    for first, at in chunks():
        pair = hidden(0, at)
        both = dot(m3[...], pair, NN)
        to_planes(both[:ROWS] + both[ROWS:] + col[:ROWS, 1:2], first, net)
    for x in range(nx):
        open_cell = fluid(x)
        for i in range(Q):
            value = f0[rows(i, x), :] + net[rows(i, x), :]
            if BUOYANCY[i] != 0.0:
                value = value + BUOYANCY[i] * t0[x]
            post[rows(i, x), :] = jnp.where(open_cell, value, f0[rows(OPPOSITE[i], x), :])
    pl.semaphore_wait(barrier, len(partners))
    copies_a = begin(0, post, 1, [lambda a, s, x: t0[x]], True)
    copies_0 = begin(1, adj2, -1, [], True)
    speeds0 = [motion(f0, x) for x in range(nx)]
    arrive(copies_a)

    def keep_f1(i, x, plane):
        f1[rows(i, x), :] = plane

    stream(post, 0, 1, keep_f1)
    for x in range(nx):
        value = (1.0 - 6.0 * CONDUCTIVITY) * t0[x]
        for a in range(3):
            for s in SIGNS:
                value = value + (CONDUCTIVITY - 0.5 * s * speeds0[x][a]) * heat_near(
                    t0, 0, 5, x, a, s
                )
        t1[x] = jnp.where(fluid(x), value, jnp.where(site[x] == 1, t0[x], HEATER))
    copies_b = begin(
        2, None, 1,
        [lambda a, s, x: t1[x], lambda a, s, x: flux(f1, tadj2, x, a, s)], False,
    )

    to_rows(f1, ft.at[1])
    for first, at in chunks():
        hidden(1, at)

    def step_back(s, fields, field, adjoint, tadj, e_adj, e_heat, heat_slot, e_flux, flux_slot,
                  waits, new_adj, new_tadj):
        lifts = [jnp.zeros((ny, nz), F32) for _ in range(nx)]

        def keep(i, x, plane):
            pcg[rows(i, x), :] = plane
            value = jnp.where(fluid(x), plane, 0.0)
            pcgf[rows(i, x), :] = value
            if BUOYANCY[i] != 0.0:
                lifts[x] = lifts[x] + BUOYANCY[i] * value

        stream(adjoint, e_adj, -1, keep)
        to_rows(pcgf, pt.at[s])
        for first, at in chunks():
            network_back(s, first, at)
        arrive(waits)
        for x in range(nx):
            wet = liquid(tadj, x)
            speed = motion(fields, x)
            value = (1.0 - 6.0 * CONDUCTIVITY) * wet + jnp.where(site[x] == 1, tadj[x], 0.0)
            for a in range(3):
                for sign in SIGNS:
                    if a == 0:
                        value = value + moved_x(
                            lambda k: flux(fields, tadj, k, 0, sign), e_flux, flux_slot, x, sign
                        )
                        continue
                    here = (CONDUCTIVITY - 0.5 * sign * speed[a]) * wet
                    if a == 1:
                        value = value + moved_y(here, face_y(e_flux, flux_slot, x, sign), sign)
                    else:
                        value = value + moved_z(here, 0.0, sign)
            new_tadj[x] = value + lifts[x]
            pulls = [
                wet * (0.5 * (heat_near(field, e_heat, heat_slot, x, a, -1)
                              - heat_near(field, e_heat, heat_slot, x, a, 1)))
                for a in range(3)
            ]
            open_cell = fluid(x)
            for i in range(Q):
                value = net[rows(i, x), :] + jnp.where(
                    open_cell, pcg[rows(i, x), :], pcg[rows(OPPOSITE[i], x), :]
                )
                for a in range(3):
                    if VELOCITIES[i, a] == 1:
                        value = value + pulls[a]
                    elif VELOCITIES[i, a] == -1:
                        value = value - pulls[a]
                new_adj[rows(i, x), :] = value

    arrive(copies_0)
    step_back(1, f1, t1, adj2, tadj2, 1, 2, 0, 2, 1, copies_b, adj1, tadj1)
    copies_c = begin(3, adj1, -1, [lambda a, s, x: flux(f0, tadj1, x, a, s)], True)
    weight_grads(1)
    arrive(copies_c)
    step_back(0, f0, t0, adj1, tadj1, 3, 0, 5, 3, 5, [], adj_out, tadj_out)
    weight_grads(0)

    part = grads.shape[0] // ngy
    if at5 + ROWS < grads.shape[0]:
        grads[at5 + ROWS :, :] = jnp.zeros((grads.shape[0] - at5 - ROWS, LANES), F32)

    def block(index):
        return pl.ds(pl.multiple_of(index * part, 8), part)

    def share(src, dst, n, dx, dy):
        c = pltpu.make_async_remote_copy(
            src_ref=src, dst_ref=dst, send_sem=gsend.at[n], recv_sem=grecv.at[n],
            device_id=device(dx, dy), device_id_type=MESH,
        )
        c.start()
        started.append(c)
        return c

    copies = []
    for d in range(1, ngy):
        copies.append(
            share(grads.at[block(lax.rem(gy + d, ngy))], parts_y.at[d - 1], d - 1, 0, d)
        )
    value = grads[block(gy), :]
    arrive(copies)
    for d in range(1, ngy):
        value = value + parts_y[d - 1]
    parts_x[0] = value
    copies = []
    for d in range(1, ngx):
        copies.append(share(parts_x.at[0], parts_x.at[d], ngy - 1 + d - 1, d, 0))
    arrive(copies)
    value = None
    for k in range(ngx):
        term = parts_x[lax.rem(gx - k + ngx, ngx)]
        value = term if value is None else value + term
    total[block(gy), :] = value
    copies = []
    for d in range(1, ngy):
        copies.append(
            share(total.at[block(gy)], total.at[block(gy)], ngy + ngx - 2 + d - 1, 0, d)
        )
    arrive(copies)
    gw1[...] = total[at1 : at1 + Q, :]
    gb1[...] = total[at1 + Q : at1 + Q + 1, :]
    gw2[...] = total[at2 : at2 + hid, :]
    gb2[...] = total[at3 : at3 + 1, :]
    square[...] = jnp.zeros_like(square)
    square[0:ROWS, :] = total[at4 : at4 + ROWS, :]
    gw3[...] = jnp.transpose(square[...])[:, 0:Q]
    square[0:ROWS, :] = total[at5 : at5 + ROWS, :]
    gb3[...] = jnp.transpose(square[...])[0:1, 0:Q]
    for c in started:
        c.wait_send()


def per_device(ngx, ngy, f0, t0, site, w1, b1, w2, b2, w3, b3, adj2, tadj2):
    q, nx, ny, nz = f0.shape
    hid = w2.shape[0]
    sites = nx * ny * nz
    flat = (q * nx * ny, nz)
    factor = 1.0 / math.sqrt(nx * ngx * ny * ngy * nz)
    needed = 3 * ROWS + hid + 8
    unit = 8 * ngy
    length = -(-needed // unit) * unit
    side = -(-(SLOTS * nx) // 8) * 8
    plane = pltpu.VMEM((nx, ny, nz), F32)
    wide = pltpu.VMEM(flat, F32)
    dma = pltpu.SemaphoreType.DMA
    gcount = 2 * (ngy - 1) + ngx - 1
    scratch = [
        wide, wide, plane, wide, plane, wide, wide, wide,
        pltpu.VMEM((2, ROWS, sites), F32),
        pltpu.VMEM((2, ROWS, sites), F32),
        pltpu.VMEM((2, hid, sites), F32),
        pltpu.VMEM((2, hid, sites), F32),
        pltpu.VMEM((2, 2 * hid, sites), BF16),
        pltpu.VMEM((2, 2 * hid, sites), BF16),
        pltpu.VMEM((2, 2 * hid, sites), BF16),
        pltpu.VMEM((2, 2 * hid, sites), BF16),
        pltpu.VMEM((hid, hid), F32),
        pltpu.VMEM((hid, 3 * ROWS), BF16),
        pltpu.VMEM((2 * hid, 2 * hid), BF16),
        pltpu.VMEM((2 * ROWS, 2 * hid), BF16),
        pltpu.VMEM((2 * ROWS, 2 * hid), BF16),
        pltpu.VMEM((2 * hid, 2 * hid), BF16),
        pltpu.VMEM((hid, 3 * ROWS), BF16),
        pltpu.VMEM((hid, hid), F32),
        pltpu.VMEM((4, 2, SLOTS * ny, nz), F32),
        pltpu.VMEM((4, 2, side, nz), F32),
        pltpu.VMEM((4, 4, 8, nz), F32),
        pltpu.VMEM((4, 2, SLOTS * ny, nz), F32),
        pltpu.VMEM((4, 2, side, nz), F32),
        pltpu.VMEM((4, 4, 8, nz), F32),
        dma((4, 8)),
        dma((4, 8)),
        pltpu.VMEM((length, LANES), F32),
        pltpu.VMEM((ngy - 1, length // ngy, LANES), F32),
        pltpu.VMEM((ngx, length // ngy, LANES), F32),
        pltpu.VMEM((length, LANES), F32),
        dma((gcount,)),
        dma((gcount,)),
    ]
    shape = jax.ShapeDtypeStruct
    vmem = pl.BlockSpec(memory_space=pltpu.VMEM)
    outs = pl.pallas_call(
        functools.partial(kernel, (nx, ny, nz, ngx, ngy, factor)),
        out_shape=[
            shape(flat, F32), shape((nx, ny, nz), F32),
            shape(w1.shape, F32), shape((1, hid), F32),
            shape(w2.shape, F32), shape((1, hid), F32),
            shape(w3.shape, F32), shape((1, q), F32),
        ],
        in_specs=[vmem] * 11,
        out_specs=[vmem] * 8,
        scratch_shapes=scratch,
        compiler_params=pltpu.CompilerParams(
            collective_id=0, has_side_effects=True, vmem_limit_bytes=48 * 1024 * 1024
        ),
    )(
        f0.reshape(flat), t0, site, w1, b1.reshape(1, hid), w2, b2.reshape(1, hid),
        w3, b3.reshape(1, q), adj2.reshape(flat), tadj2,
    )
    return (
        outs[0].reshape(f0.shape), outs[1], outs[2], outs[3].reshape(hid),
        outs[4], outs[5].reshape(hid), outs[6], outs[7].reshape(q),
    )


def solution(mesh):
    grid = P(None, "gx", "gy", None)
    plane = P("gx", "gy", None)
    in_specs = (grid, plane, plane) + (P(),) * 6 + (grid, plane)
    out_specs = (grid, plane) + (P(),) * 6
    return jax.shard_map(
        functools.partial(per_device, mesh.shape["gx"], mesh.shape["gy"]),
        mesh=mesh, in_specs=in_specs, out_specs=out_specs, check_vma=False,
    )
```

```python
import functools
import math

import jax
import jax.numpy as jnp
import numpy as np
from jax import lax
from jax.experimental import pallas as pl
from jax.experimental.pallas import tpu as pltpu
from jax.sharding import PartitionSpec as P

VELOCITIES = np.array(
    [
        [0, 0, 0],
        [1, 0, 0],
        [-1, 0, 0],
        [0, 1, 0],
        [0, -1, 0],
        [0, 0, 1],
        [0, 0, -1],
        [1, 1, 0],
        [-1, -1, 0],
        [1, -1, 0],
        [-1, 1, 0],
        [1, 0, 1],
        [-1, 0, -1],
        [1, 0, -1],
        [-1, 0, 1],
        [0, 1, 1],
        [0, -1, -1],
        [0, 1, -1],
        [0, -1, 1],
    ]
)
Q = len(VELOCITIES)
OPPOSITE = [0, 2, 1, 4, 3, 6, 5, 8, 7, 10, 9, 12, 11, 14, 13, 16, 15, 18, 17]
LATTICE_WEIGHTS = np.array([1.0 / 3.0] + [1.0 / 18.0] * 6 + [1.0 / 36.0] * 12)
BUOYANCY = [float(v) for v in 0.3 * LATTICE_WEIGHTS * VELOCITIES[:, 2]]
CONDUCTIVITY = 0.1
HOT_WALL = 0.5
COLD_WALL = -0.5
HEATER = 0.5
SIGNS = (1, -1)
CORNERS = [(1, 1), (1, -1), (-1, 1), (-1, -1)]
LANES = 128
ROWS = 32
SLOTS = 6
MESH = pl.DeviceIdType.MESH
BF16 = jnp.bfloat16
F32 = jnp.float32
NN = (((1,), (0,)), ((), ()))
NT = (((1,), (1,)), ((), ()))


def steps_of(orient):
    return [tuple(int(v) * orient for v in VELOCITIES[i]) for i in range(Q)]


def movers(orient, axis, sign):
    return [i for i, step in enumerate(steps_of(orient)) if step[axis] == sign]


def corner_mover(orient, dx, dy):
    return steps_of(orient).index((dx, dy, 0))


def halves(values):
    high = values.astype(BF16)
    return high, (values - high.astype(F32)).astype(BF16)


def dot(a, b, dims):
    return lax.dot_general(a, b, dims, preferred_element_type=F32)


def kernel(
    sizes,
    f0_in, t0_in, site_in, w1_in, b1_in, w2_in, b2_in, w3_in, b3_in, adj2_in, tadj2_in,
    adj_to, tadj_to, gw1_to, gb1_to, gw2_to, gb2_to, gw3_to, gb3_to,
    adj_out, tadj_out, gw1, gb1, gw2, gb2, gw3, gb3, stored,
    f0, t0, site, w1, b1, w2, b2, w3, b3, adj2, tadj2, loaded,
    post, f1, t1, adj1, tadj1, net, pcg, pcgf,
    ft, pt, back, h1, h2, h1c, h2c, d1c, d2c,
    square, m1, m2, m3, r1, r2, r3, col,
    sx, sy, sc, rx, ry, rc, send, recv,
    grads, parts_y, parts_x, total, gsend, grecv,
):
    nx, ny, nz, ngx, ngy, factor = sizes
    cols = nx * ny
    sites = cols * nz
    hid = w2.shape[0]
    chunk = min(4, cols)
    gx, gy = lax.axis_index("gx"), lax.axis_index("gy")
    arguments = [
        (w1_in, w1), (b1_in, b1), (w2_in, w2), (b2_in, b2), (w3_in, w3), (b3_in, b3),
        (f0_in, f0), (t0_in, t0), (site_in, site), (adj2_in, adj2), (tadj2_in, tadj2),
    ]
    loads = [
        pltpu.make_async_copy(src, dst, loaded.at[k]) for k, (src, dst) in enumerate(arguments)
    ]
    for c in loads:
        c.start()

    def device(dx, dy):
        return (lax.rem(gx + dx + ngx, ngx), lax.rem(gy + dy + ngy, ngy))

    barrier = pltpu.get_barrier_semaphore()
    duo = 2 if ngx % 2 == 0 else 1
    spot = lax.rem(gx, duo)

    def near(dx, dy):
        return (gx - spot + lax.rem(spot + dx, duo), lax.rem(gy + dy, ngy))

    inner = [(dx, dy) for dx in range(duo) for dy in range(ngy)][1:]
    outer = ngx // duo
    partners = [device(dx, dy) for dx, dy in [(1, 0), (-1, 0), (0, 1), (0, -1)] + CORNERS]
    partners += [near(dx, dy) for dx, dy in inner]
    partners += [device(duo * d, 0) for d in range(1, outer)]
    for partner in partners:
        pl.semaphore_signal(barrier, inc=1, device_id=partner, device_id_type=MESH)

    def rows(i, x):
        return pl.ds((i * nx + x) * ny, ny)

    def row(i, x, y):
        return pl.ds((i * nx + x) * ny + y, 1)

    depth = lax.broadcasted_iota(jnp.int32, (ny, nz), 1)
    height = lax.broadcasted_iota(jnp.int32, (ny, nz), 0)

    for s in range(2):
        ft[s] = jnp.zeros((ROWS, sites), F32)
        ft[s, Q : Q + 1, :] = jnp.ones((1, sites), F32)
    pt[...] = jnp.zeros_like(pt)
    grads[...] = jnp.zeros_like(grads)
    square[...] = jnp.zeros_like(square)
    for c in loads[:6]:
        c.wait()
    square[0:Q, :] = w1[...]
    square[Q : Q + 1, :] = b1[...]
    w1_rows = square[...]
    a, b = halves(jnp.transpose(w1_rows)[:, :ROWS])
    m1[...] = jnp.concatenate([a, a, b], axis=1)
    a, b = halves(w1_rows[:ROWS])
    r1[...] = jnp.concatenate(
        [jnp.concatenate([a, a], axis=1), jnp.concatenate([b, jnp.zeros_like(b)], axis=1)], axis=0
    )
    for matrix, target in ((jnp.transpose(w2[...]), m2), (w2[...], r2)):
        a, b = halves(matrix)
        target[...] = jnp.concatenate(
            [jnp.concatenate([a, a], axis=1), jnp.concatenate([b, jnp.zeros_like(b)], axis=1)],
            axis=0,
        )
    square[...] = jnp.zeros_like(square)
    square[0:Q, :] = w3[...]
    w3_rows = square[...]
    a, b = halves(w3_rows[:ROWS])
    m3[...] = jnp.concatenate(
        [jnp.concatenate([a, a], axis=1), jnp.concatenate([b, jnp.zeros_like(b)], axis=1)], axis=0
    )
    a, b = halves(jnp.transpose(w3_rows)[:, :ROWS])
    r3[...] = jnp.concatenate([a, a, b], axis=1)
    square[...] = jnp.zeros_like(square)
    square[0:1, :] = b2[...]
    square[1:2, 0:Q] = b3[...]
    col[...] = jnp.transpose(square[...])

    def to_rows(source, target):
        for c in range(cols):
            target[0:Q, c * nz : (c + 1) * nz] = source[pl.ds(c, Q, stride=cols), :]

    def to_planes(values, first, target):
        for c in range(chunk):
            target[pl.ds(first + c, Q, stride=cols), :] = values[0:Q, c * nz : (c + 1) * nz]

    def chunks():
        for first in range(0, cols, chunk):
            yield first, pl.ds(first * nz, chunk * nz)

    def hidden(s, at):
        a, b = halves(ft[s, :, at])
        one = jnp.tanh(dot(m1[...], jnp.concatenate([a, b, a], axis=0), NN))
        h1[s, :, at] = one
        pair = jnp.concatenate(halves(one), axis=0)
        h1c[s, :, at] = pair
        both = dot(m2[...], pair, NN)
        two = jnp.tanh(both[:hid] + both[hid:] + col[:, 0:1])
        h2[s, :, at] = two
        pair = jnp.concatenate(halves(two), axis=0)
        h2c[s, :, at] = pair
        return pair

    def network_back(s, at):
        two = h2[s, :, at]
        pair = jnp.concatenate(halves(back[:, at] * (1.0 - two * two)), axis=0)
        d2c[s, :, at] = pair
        both = dot(r2[...], pair, NN)
        one = h1[s, :, at]
        pair = jnp.concatenate(halves((both[:hid] + both[hid:]) * (1.0 - one * one)), axis=0)
        d1c[s, :, at] = pair

    def network_in(s):
        for first, at in chunks():
            both = dot(r1[...], d1c[s, :, at], NN)
            to_planes(both[:ROWS] + both[ROWS:], first, net)

    def folded(product, n, m):
        return product[:n, :m] + product[:n, m : 2 * m] + product[n : 2 * n, :m]

    at2 = 24
    at3 = at2 + hid
    at4 = at3 + Q

    def weight_grads(s):
        ones = jnp.ones((16, sites), BF16)
        pairs = dot(jnp.concatenate(halves(ft[s]), axis=0), d1c[s], NT)
        first = folded(pairs, ROWS, hid)[: Q + 1]
        pairs = dot(jnp.concatenate([h1c[s], ones], axis=0), d2c[s], NT)
        second = folded(pairs, hid, hid)
        second_bias = (pairs[2 * hid :, :hid] + pairs[2 * hid :, hid:])[0:1]
        split = jnp.concatenate(halves(pt[s]), axis=0)
        third = folded(dot(split, h2c[s], NT), ROWS, hid)[:Q]
        pairs = dot(ones, split, NT)
        third_bias = (pairs[:, :ROWS] + pairs[:, ROWS:])[0:1]
        for start, value in (
            (0, first), (at2, second), (at3, third), (at4, second_bias), (at4 + 1, third_bias)
        ):
            n, m = value.shape
            if s == 1:
                grads[start : start + n, :m] = value
            else:
                grads[start : start + n, :m] = (grads[start : start + n, :m] + value) * factor

    started = []

    def begin(e, source, orient, extras, corners):
        found = {}
        for k, sign in enumerate(SIGNS):
            slot = 0
            for i in movers(orient, 0, sign) if source is not None else ():
                sx[e, k, slot * ny : (slot + 1) * ny, :] = source[
                    rows(i, nx - 1 if sign == 1 else 0), :
                ]
                slot += 1
            for extra in extras:
                sx[e, k, slot * ny : (slot + 1) * ny, :] = extra(
                    0, sign, nx - 1 if sign == 1 else 0
                )
                slot += 1
            slot = 0
            edge = ny - 1 if sign == 1 else 0
            for i in movers(orient, 1, sign) if source is not None else ():
                for x in range(nx):
                    sy[e, k, slot * nx + x : slot * nx + x + 1, :] = source[row(i, x, edge), :]
                slot += 1
            for extra in extras:
                for x in range(nx):
                    sy[e, k, slot * nx + x : slot * nx + x + 1, :] = extra(1, sign, x)[
                        edge : edge + 1, :
                    ]
                slot += 1
        if corners:
            for k, (dx, dy) in enumerate(CORNERS):
                i = corner_mover(orient, dx, dy)
                sc[e, k, 0:1, :] = source[
                    row(i, nx - 1 if dx == 1 else 0, ny - 1 if dy == 1 else 0), :
                ]

        def copy(src, dst, n, dx, dy):
            found[n] = pltpu.make_async_remote_copy(
                src_ref=src, dst_ref=dst, send_sem=send.at[e, n], recv_sem=recv.at[e, n],
                device_id=device(dx, dy), device_id_type=MESH,
            )
            found[n].start()

        for k, sign in enumerate(SIGNS):
            copy(sx.at[e, k], rx.at[e, k], k, sign, 0)
            copy(sy.at[e, k], ry.at[e, k], 2 + k, 0, sign)
        if corners:
            for k, (dx, dy) in enumerate(CORNERS):
                copy(sc.at[e, k], rc.at[e, k], 4 + k, dx, dy)
        started.extend(found.values())
        return list(found.values())

    def arrive(copies):
        for c in copies:
            c.wait_recv()

    def moved_x(inside, e, slot, x, sign):
        if 0 <= x - sign < nx:
            return inside(x - sign)
        return rx[e, SIGNS.index(sign), slot * ny : (slot + 1) * ny, :]

    def moved_y(plane, edge_row, sign):
        shifted = pltpu.roll(plane, 1 if sign == 1 else ny - 1, 0)
        edge = 0 if sign == 1 else ny - 1
        return jnp.where(height == edge, jnp.broadcast_to(edge_row, shifted.shape), shifted)

    def moved_z(plane, fill, sign):
        shifted = pltpu.roll(plane, 1 if sign == 1 else nz - 1, 1)
        return jnp.where(depth == (0 if sign == 1 else nz - 1), fill, shifted)

    def face_y(e, slot, x, sign):
        at = slot * nx + x
        return ry[e, SIGNS.index(sign), at : at + 1, :]

    def stream(source, e, orient, store):
        for i, (px, py, pz) in enumerate(steps_of(orient)):
            for x in range(nx):
                plane = None
                if px:
                    plane = moved_x(
                        lambda k: source[rows(i, k), :],
                        e, movers(orient, 0, px).index(i), x, px,
                    )
                else:
                    plane = source[rows(i, x), :]
                if py:
                    if 0 <= x - px < nx:
                        edge = face_y(e, movers(orient, 1, py).index(i), x - px, py)
                    else:
                        edge = rc[e, CORNERS.index((px, py)), 0:1, :]
                    plane = moved_y(plane, edge, py)
                if pz:
                    plane = moved_z(plane, source[rows(OPPOSITE[i], x), :], pz)
                store(i, x, plane)

    def motion(fields, x):
        result = []
        for a in range(3):
            value = None
            for i in range(Q):
                if VELOCITIES[i, a] == 0:
                    continue
                term = fields[rows(i, x), :]
                if value is None:
                    value = term if VELOCITIES[i, a] == 1 else -term
                elif VELOCITIES[i, a] == 1:
                    value = value + term
                else:
                    value = value - term
            result.append(value)
        return result

    def heat_near(field, e, slot, x, a, s):
        if a == 0:
            return moved_x(lambda k: field[k], e, slot, x, -s)
        if a == 1:
            return moved_y(field[x], face_y(e, slot, x, -s), -s)
        return moved_z(field[x], COLD_WALL if s == 1 else HOT_WALL, -s)

    def fluid(x):
        return site[x] == 0

    def liquid(tadj, x):
        return jnp.where(fluid(x), tadj[x], 0.0)

    def flux(fields, tadj, x, a, s):
        return (CONDUCTIVITY - 0.5 * s * motion(fields, x)[a]) * liquid(tadj, x)

    loads[6].wait()
    to_rows(f0, ft.at[0])
    halfway = (cols // chunk) // 2 * chunk
    for first, at in chunks():
        if first == halfway:
            loads[9].wait()
            pl.semaphore_wait(barrier, len(partners))
            copies_0 = begin(1, adj2, -1, [], True)
        pair = hidden(0, at)
        both = dot(m3[...], pair, NN)
        to_planes(both[:ROWS] + both[ROWS:] + col[:ROWS, 1:2], first, net)
    for c in loads[7:9] + loads[10:]:
        c.wait()
    for x in range(nx):
        open_cell = fluid(x)
        for i in range(Q):
            value = f0[rows(i, x), :] + net[rows(i, x), :]
            if BUOYANCY[i] != 0.0:
                value = value + BUOYANCY[i] * t0[x]
            post[rows(i, x), :] = jnp.where(open_cell, value, f0[rows(OPPOSITE[i], x), :])
    copies_a = begin(0, post, 1, [lambda a, s, x: t0[x]], True)

    def incoming(s, adjoint, e_adj):
        lifts = [jnp.zeros((ny, nz), F32) for _ in range(nx)]

        def keep(i, x, plane):
            pcg[rows(i, x), :] = plane
            value = jnp.where(fluid(x), plane, 0.0)
            pcgf[rows(i, x), :] = value
            if BUOYANCY[i] != 0.0:
                lifts[x] = lifts[x] + BUOYANCY[i] * value

        stream(adjoint, e_adj, -1, keep)
        to_rows(pcgf, pt.at[s])
        for first, at in chunks():
            a, b = halves(pt[s, :, at])
            back[:, at] = dot(r3[...], jnp.concatenate([a, b, a], axis=0), NN)
        return lifts

    speeds0 = [motion(f0, x) for x in range(nx)]
    arrive(copies_0)
    lifts = incoming(1, adj2, 1)
    arrive(copies_a)

    def keep_f1(i, x, plane):
        f1[rows(i, x), :] = plane

    stream(post, 0, 1, keep_f1)
    for x in range(nx):
        value = (1.0 - 6.0 * CONDUCTIVITY) * t0[x]
        for a in range(3):
            for s in SIGNS:
                value = value + (CONDUCTIVITY - 0.5 * s * speeds0[x][a]) * heat_near(
                    t0, 0, 5, x, a, s
                )
        t1[x] = jnp.where(fluid(x), value, jnp.where(site[x] == 1, t0[x], HEATER))
    copies_b = begin(
        2, None, 1,
        [lambda a, s, x: t1[x], lambda a, s, x: flux(f1, tadj2, x, a, s)], False,
    )

    to_rows(f1, ft.at[1])
    for first, at in chunks():
        hidden(1, at)
        network_back(1, at)

    def assemble(fields, field, tadj, e_heat, heat_slot, e_flux, flux_slot, lifts, new_adj,
                 new_tadj):
        for x in range(nx):
            wet = liquid(tadj, x)
            speed = motion(fields, x)
            value = (1.0 - 6.0 * CONDUCTIVITY) * wet + jnp.where(site[x] == 1, tadj[x], 0.0)
            for a in range(3):
                for sign in SIGNS:
                    if a == 0:
                        value = value + moved_x(
                            lambda k: flux(fields, tadj, k, 0, sign), e_flux, flux_slot, x, sign
                        )
                        continue
                    here = (CONDUCTIVITY - 0.5 * sign * speed[a]) * wet
                    if a == 1:
                        value = value + moved_y(here, face_y(e_flux, flux_slot, x, sign), sign)
                    else:
                        value = value + moved_z(here, 0.0, sign)
            new_tadj[x] = value + lifts[x]
            pulls = [
                wet * (0.5 * (heat_near(field, e_heat, heat_slot, x, a, -1)
                              - heat_near(field, e_heat, heat_slot, x, a, 1)))
                for a in range(3)
            ]
            open_cell = fluid(x)
            for i in range(Q):
                value = net[rows(i, x), :] + jnp.where(
                    open_cell, pcg[rows(i, x), :], pcg[rows(OPPOSITE[i], x), :]
                )
                for a in range(3):
                    if VELOCITIES[i, a] == 1:
                        value = value + pulls[a]
                    elif VELOCITIES[i, a] == -1:
                        value = value - pulls[a]
                new_adj[rows(i, x), :] = value

    network_in(1)
    arrive(copies_b)
    assemble(f1, t1, tadj2, 2, 0, 2, 1, lifts, adj1, tadj1)
    copies_c = begin(3, adj1, -1, [lambda a, s, x: flux(f0, tadj1, x, a, s)], True)
    weight_grads(1)
    arrive(copies_c)
    lifts = incoming(0, adj1, 3)
    for first, at in chunks():
        network_back(0, at)
    results = [
        (adj_out, adj_to), (tadj_out, tadj_to), (gw1, gw1_to), (gb1, gb1_to),
        (gw2, gw2_to), (gb2, gb2_to), (gw3, gw3_to), (gb3, gb3_to),
    ]
    stores = [
        pltpu.make_async_copy(src, dst, stored.at[k]) for k, (src, dst) in enumerate(results)
    ]
    weight_grads(0)

    part = grads.shape[0] // (duo * ngy)

    def block(where):
        index = (where[0] - (gx - spot)) * ngy + where[1]
        return pl.ds(pl.multiple_of(index * part, 8), part)

    def share(src, dst, n, target):
        c = pltpu.make_async_remote_copy(
            src_ref=src, dst_ref=dst, send_sem=gsend.at[n], recv_sem=grecv.at[n],
            device_id=target, device_id_type=MESH,
        )
        c.start()
        started.append(c)
        return c

    mine = block((gx, gy))
    copies = []
    for n, (dx, dy) in enumerate(inner):
        copies.append(share(grads.at[block(near(dx, dy))], parts_y.at[n], n, near(dx, dy)))
    network_in(0)
    assemble(f0, t0, tadj1, 0, 5, 3, 5, lifts, adj_out, tadj_out)
    for c in stores[:2]:
        c.start()
    value = grads[mine, :]
    for n, c in enumerate(copies):
        c.wait_recv()
        value = value + parts_y[n]
    parts_x[0] = value
    copies = []
    for d in range(1, outer):
        copies.append(
            share(parts_x.at[0], parts_x.at[d], len(inner) + d - 1, device(duo * d, 0))
        )
    arrive(copies)
    value = None
    for k in range(outer):
        term = parts_x[lax.rem((gx - spot) // duo - k + outer, outer)]
        value = term if value is None else value + term
    total[mine, :] = value
    copies = []
    for n, (dx, dy) in enumerate(inner):
        copies.append(
            share(total.at[mine], total.at[mine], len(inner) + outer - 1 + n, near(dx, dy))
        )
    arrive(copies)
    gw1[...] = total[0:Q, :]
    gb1[...] = total[Q : Q + 1, :]
    gw2[...] = total[at2 : at2 + hid, :]
    gw3[...] = total[at3 : at3 + Q, :]
    gb2[...] = total[at4 : at4 + 1, :]
    gb3[...] = total[at4 + 1 : at4 + 2, 0:Q]
    for c in stores[2:]:
        c.start()
    for c in started:
        c.wait_send()
    for c in stores:
        c.wait()


def hand_out(*refs):
    load, store = refs[-2:]
    n = (len(refs) - 2) // 3
    ins, outs, held = refs[:n], refs[n : 2 * n], refs[2 * n : 3 * n]
    loads = [pltpu.make_async_copy(ins[k], held[k], load.at[k]) for k in range(n)]
    stores = [pltpu.make_async_copy(held[k], outs[k], store.at[k]) for k in range(n)]
    for c in loads:
        c.start()
    for k in range(n):
        loads[k].wait()
        stores[k].start()
    for c in stores:
        c.wait()


def per_device(ngx, ngy, f0, t0, site, w1, b1, w2, b2, w3, b3, adj2, tadj2):
    q, nx, ny, nz = f0.shape
    hid = w2.shape[0]
    sites = nx * ny * nz
    flat = (q * nx * ny, nz)
    factor = 1.0 / math.sqrt(nx * ngx * ny * ngy * nz)
    group = (2 if ngx % 2 == 0 else 1) * ngy
    outer = ngx * ngy // group
    needed = 24 + hid + 24
    unit = 8 * group
    length = -(-needed // unit) * unit
    side = -(-(SLOTS * nx) // 8) * 8
    plane = pltpu.VMEM((nx, ny, nz), F32)
    wide = pltpu.VMEM(flat, F32)
    dma = pltpu.SemaphoreType.DMA
    gcount = 2 * (group - 1) + outer - 1
    scratch = [
        wide, plane, pltpu.VMEM(w1.shape, F32), pltpu.VMEM((1, hid), F32),
        pltpu.VMEM(w2.shape, F32), pltpu.VMEM((1, hid), F32),
        pltpu.VMEM((q, hid), F32), pltpu.VMEM((1, q), F32), dma((8,)),
        wide, plane, pltpu.VMEM((nx, ny, nz), jnp.int32),
        pltpu.VMEM(w1.shape, F32), pltpu.VMEM((1, hid), F32),
        pltpu.VMEM(w2.shape, F32), pltpu.VMEM((1, hid), F32),
        pltpu.VMEM((q, hid), F32), pltpu.VMEM((1, q), F32),
        wide, plane, dma((11,)),
        wide, wide, plane, wide, plane, wide, wide, wide,
        pltpu.VMEM((2, ROWS, sites), F32),
        pltpu.VMEM((2, ROWS, sites), F32),
        pltpu.VMEM((hid, sites), F32),
        pltpu.VMEM((2, hid, sites), F32),
        pltpu.VMEM((2, hid, sites), F32),
        pltpu.VMEM((2, 2 * hid, sites), BF16),
        pltpu.VMEM((2, 2 * hid, sites), BF16),
        pltpu.VMEM((2, 2 * hid, sites), BF16),
        pltpu.VMEM((2, 2 * hid, sites), BF16),
        pltpu.VMEM((hid, hid), F32),
        pltpu.VMEM((hid, 3 * ROWS), BF16),
        pltpu.VMEM((2 * hid, 2 * hid), BF16),
        pltpu.VMEM((2 * ROWS, 2 * hid), BF16),
        pltpu.VMEM((2 * ROWS, 2 * hid), BF16),
        pltpu.VMEM((2 * hid, 2 * hid), BF16),
        pltpu.VMEM((hid, 3 * ROWS), BF16),
        pltpu.VMEM((hid, hid), F32),
        pltpu.VMEM((4, 2, SLOTS * ny, nz), F32),
        pltpu.VMEM((4, 2, side, nz), F32),
        pltpu.VMEM((4, 4, 8, nz), F32),
        pltpu.VMEM((4, 2, SLOTS * ny, nz), F32),
        pltpu.VMEM((4, 2, side, nz), F32),
        pltpu.VMEM((4, 4, 8, nz), F32),
        dma((4, 8)),
        dma((4, 8)),
        pltpu.VMEM((length, LANES), F32),
        pltpu.VMEM((group - 1, length // group, LANES), F32),
        pltpu.VMEM((outer, length // group, LANES), F32),
        pltpu.VMEM((length, LANES), F32),
        dma((gcount,)),
        dma((gcount,)),
    ]
    shape = jax.ShapeDtypeStruct
    anywhere = pl.BlockSpec(memory_space=pltpu.HBM)
    shapes = [
        shape(flat, F32), shape((nx, ny, nz), F32),
        shape(w1.shape, F32), shape((1, hid), F32),
        shape(w2.shape, F32), shape((1, hid), F32),
        shape((q, hid), F32), shape((1, q), F32),
    ]
    outs = pl.pallas_call(
        functools.partial(kernel, (nx, ny, nz, ngx, ngy, factor)),
        out_shape=shapes,
        in_specs=[anywhere] * 11,
        out_specs=[anywhere] * 8,
        scratch_shapes=scratch,
        compiler_params=pltpu.CompilerParams(
            collective_id=0, has_side_effects=True, vmem_limit_bytes=64 * 1024 * 1024
        ),
    )(
        f0.reshape(flat), t0, site, w1, b1.reshape(1, hid), w2, b2.reshape(1, hid),
        w3.T, b3.reshape(1, q), adj2.reshape(flat), tadj2,
    )
    outs = pl.pallas_call(
        hand_out,
        out_shape=shapes,
        in_specs=[anywhere] * 8,
        out_specs=[anywhere] * 8,
        scratch_shapes=[pltpu.VMEM(s.shape, s.dtype) for s in shapes] + [dma((8,)), dma((8,))],
        compiler_params=pltpu.CompilerParams(vmem_limit_bytes=64 * 1024 * 1024),
    )(*outs)
    return (
        outs[0].reshape(f0.shape), outs[1], outs[2], outs[3].reshape(hid),
        outs[4], outs[5].reshape(hid), outs[6].T, outs[7].reshape(q),
    )


def solution(mesh):
    grid = P(None, "gx", "gy", None)
    plane = P("gx", "gy", None)
    in_specs = (grid, plane, plane) + (P(),) * 6 + (grid, plane)
    out_specs = (grid, plane) + (P(),) * 6
    return jax.shard_map(
        functools.partial(per_device, mesh.shape["gx"], mesh.shape["gy"]),
        mesh=mesh, in_specs=in_specs, out_specs=out_specs, check_vma=False,
    )
```

```python
import functools
import math

import jax
import jax.numpy as jnp
import numpy as np
from jax import lax
from jax.experimental import pallas as pl
from jax.experimental.pallas import tpu as pltpu
from jax.sharding import PartitionSpec as P

VELOCITIES = np.array(
    [
        [0, 0, 0],
        [1, 0, 0],
        [-1, 0, 0],
        [0, 1, 0],
        [0, -1, 0],
        [0, 0, 1],
        [0, 0, -1],
        [1, 1, 0],
        [-1, -1, 0],
        [1, -1, 0],
        [-1, 1, 0],
        [1, 0, 1],
        [-1, 0, -1],
        [1, 0, -1],
        [-1, 0, 1],
        [0, 1, 1],
        [0, -1, -1],
        [0, 1, -1],
        [0, -1, 1],
    ]
)
Q = len(VELOCITIES)
OPPOSITE = [0, 2, 1, 4, 3, 6, 5, 8, 7, 10, 9, 12, 11, 14, 13, 16, 15, 18, 17]
LATTICE_WEIGHTS = np.array([1.0 / 3.0] + [1.0 / 18.0] * 6 + [1.0 / 36.0] * 12)
BUOYANCY = [float(v) for v in 0.3 * LATTICE_WEIGHTS * VELOCITIES[:, 2]]
CONDUCTIVITY = 0.1
HOT_WALL = 0.5
COLD_WALL = -0.5
HEATER = 0.5
SIGNS = (1, -1)
CORNERS = [(1, 1), (1, -1), (-1, 1), (-1, -1)]
LANES = 128
ROWS = 32
SLOTS = 6
MESH = pl.DeviceIdType.MESH
BF16 = jnp.bfloat16
F32 = jnp.float32
NN = (((1,), (0,)), ((), ()))
NT = (((1,), (1,)), ((), ()))


def steps_of(orient):
    return [tuple(int(v) * orient for v in VELOCITIES[i]) for i in range(Q)]


def movers(orient, axis, sign):
    return [i for i, step in enumerate(steps_of(orient)) if step[axis] == sign]


def corner_mover(orient, dx, dy):
    return steps_of(orient).index((dx, dy, 0))


def halves(values):
    high = values.astype(BF16)
    return high, (values - high.astype(F32)).astype(BF16)


def dot(a, b, dims):
    return lax.dot_general(a, b, dims, preferred_element_type=F32)


def kernel(
    sizes,
    f0_in, t0_in, site_in, w1_in, b1_in, w2_in, b2_in, w3_in, b3_in, adj2_in, tadj2_in,
    adj_to, tadj_to, gw1_to, gb1_to, gw2_to, gb2_to, gw3_to, gb3_to,
    adj_out, tadj_out, gw1, gb1, gw2, gb2, gw3, gb3, stored,
    f0, t0, site, w1, b1, w2, b2, w3, b3, adj2, tadj2, loaded,
    post, f1, t1, adj1, tadj1, net, pcg, pcgf,
    ft, pt, back, h1, h2, h1c, h2c, d1c, d2c,
    square, m1, m2, m3, r1, r2, r3, col,
    sx, sy, sc, rx, ry, rc, send, recv,
    grads, parts_y, parts_x, total, gsend, grecv,
):
    nx, ny, nz, ngx, ngy, factor = sizes
    cols = nx * ny
    sites = cols * nz
    hid = w2.shape[0]
    gx, gy = lax.axis_index("gx"), lax.axis_index("gy")
    arguments = [
        (w1_in, w1), (b1_in, b1), (w2_in, w2), (b2_in, b2), (w3_in, w3), (b3_in, b3),
        (f0_in, f0), (t0_in, t0), (site_in, site), (adj2_in, adj2), (tadj2_in, tadj2),
    ]
    loads = [
        pltpu.make_async_copy(src, dst, loaded.at[k]) for k, (src, dst) in enumerate(arguments)
    ]
    for c in loads:
        c.start()

    def device(dx, dy):
        return (lax.rem(gx + dx + ngx, ngx), lax.rem(gy + dy + ngy, ngy))

    barrier = pltpu.get_barrier_semaphore()
    duo = 2 if ngx % 2 == 0 else 1
    spot = lax.rem(gx, duo)

    def near(dx, dy):
        return (gx - spot + lax.rem(spot + dx, duo), lax.rem(gy + dy, ngy))

    inner = [(dx, dy) for dx in range(duo) for dy in range(ngy)][1:]
    outer = ngx // duo
    partners = [device(dx, dy) for dx, dy in [(1, 0), (-1, 0), (0, 1), (0, -1)] + CORNERS]
    partners += [near(dx, dy) for dx, dy in inner]
    partners += [device(duo * d, 0) for d in range(1, outer)]
    for partner in partners:
        pl.semaphore_signal(barrier, inc=1, device_id=partner, device_id_type=MESH)

    def rows(i, x):
        return pl.ds((i * nx + x) * ny, ny)

    def row(i, x, y):
        return pl.ds((i * nx + x) * ny + y, 1)

    depth = lax.broadcasted_iota(jnp.int32, (ny, nz), 1)
    height = lax.broadcasted_iota(jnp.int32, (ny, nz), 0)

    for s in range(2):
        ft[s] = jnp.zeros((ROWS, sites), F32)
        ft[s, Q : Q + 1, :] = jnp.ones((1, sites), F32)
        h1c[s, 2 * hid :, :] = jnp.ones((16, sites), BF16)
    pt[...] = jnp.zeros_like(pt)
    grads[...] = jnp.zeros_like(grads)
    square[...] = jnp.zeros_like(square)
    for c in loads[:6]:
        c.wait()
    square[0:Q, :] = w1[...]
    square[Q : Q + 1, :] = b1[...]
    w1_rows = square[...]
    a, b = halves(jnp.transpose(w1_rows)[:, :ROWS])
    m1[...] = jnp.concatenate([a, a, b], axis=1)
    a, b = halves(w1_rows[:ROWS])
    r1[...] = jnp.concatenate(
        [jnp.concatenate([a, a], axis=1), jnp.concatenate([b, jnp.zeros_like(b)], axis=1)], axis=0
    )
    for matrix, target in ((jnp.transpose(w2[...]), m2), (w2[...], r2)):
        a, b = halves(matrix)
        target[...] = jnp.concatenate(
            [jnp.concatenate([a, a], axis=1), jnp.concatenate([b, jnp.zeros_like(b)], axis=1)],
            axis=0,
        )
    square[...] = jnp.zeros_like(square)
    square[0:Q, :] = w3[...]
    w3_rows = square[...]
    a, b = halves(w3_rows[:ROWS])
    m3[...] = jnp.concatenate(
        [jnp.concatenate([a, a], axis=1), jnp.concatenate([b, jnp.zeros_like(b)], axis=1)], axis=0
    )
    a, b = halves(jnp.transpose(w3_rows)[:, :ROWS])
    r3[...] = jnp.concatenate([a, a, b], axis=1)
    square[...] = jnp.zeros_like(square)
    square[0:1, :] = b2[...]
    square[1:2, 0:Q] = b3[...]
    col[...] = jnp.transpose(square[...])

    def to_rows(source, target):
        for c in range(cols):
            target[0:Q, c * nz : (c + 1) * nz] = source[pl.ds(c, Q, stride=cols), :]

    def to_planes(values, first, target):
        for c in range(values.shape[1] // nz):
            target[pl.ds(first + c, Q, stride=cols), :] = values[0:Q, c * nz : (c + 1) * nz]

    def chunks(chunk=cols):
        for first in range(0, cols, chunk):
            yield first, pl.ds(first * nz, chunk * nz)

    def hidden(s, at):
        a, b = halves(ft[s, :, at])
        one = jnp.tanh(dot(m1[...], jnp.concatenate([a, b, a], axis=0), NN))
        h1[s, :, at] = one
        pair = jnp.concatenate(halves(one), axis=0)
        h1c[s, 0 : 2 * hid, at] = pair
        both = dot(m2[...], pair, NN)
        two = jnp.tanh(both[:hid] + both[hid:] + col[:, 0:1])
        h2[s, :, at] = two
        pair = jnp.concatenate(halves(two), axis=0)
        h2c[s, :, at] = pair
        return pair

    def network_back(s, at):
        two = h2[s, :, at]
        pair = jnp.concatenate(halves(back[:, at] * (1.0 - two * two)), axis=0)
        d2c[s, :, at] = pair
        both = dot(r2[...], pair, NN)
        one = h1[s, :, at]
        pair = jnp.concatenate(halves((both[:hid] + both[hid:]) * (1.0 - one * one)), axis=0)
        d1c[s, :, at] = pair

    def network_in(s):
        for first, at in chunks():
            both = dot(r1[...], d1c[s, :, at], NN)
            to_planes(both[:ROWS] + both[ROWS:], first, net)

    def folded(product, n, m):
        return product[:n, :m] + product[:n, m : 2 * m] + product[n : 2 * n, :m]

    at2 = 24
    at3 = at2 + hid
    at4 = at3 + Q

    def weight_grads(s):
        ones = h1c[s, 2 * hid :, :]
        pairs = dot(jnp.concatenate(halves(ft[s]), axis=0), d1c[s], NT)
        first = folded(pairs, ROWS, hid)[: Q + 1]
        pairs = dot(h1c[s], d2c[s], NT)
        second = folded(pairs, hid, hid)
        second_bias = (pairs[2 * hid :, :hid] + pairs[2 * hid :, hid:])[0:1]
        split = jnp.concatenate(halves(pt[s]), axis=0)
        third = folded(dot(split, h2c[s], NT), ROWS, hid)[:Q]
        pairs = dot(ones, split, NT)
        third_bias = (pairs[:, :ROWS] + pairs[:, ROWS:])[0:1]
        for start, value in (
            (0, first), (at2, second), (at3, third), (at4, second_bias), (at4 + 1, third_bias)
        ):
            n, m = value.shape
            if s == 1:
                grads[start : start + n, :m] = value
            else:
                grads[start : start + n, :m] = (grads[start : start + n, :m] + value) * factor

    started = []

    def begin(e, source, orient, extras, corners):
        found = {}
        for k, sign in enumerate(SIGNS):
            slot = 0
            for i in movers(orient, 0, sign) if source is not None else ():
                sx[e, k, slot * ny : (slot + 1) * ny, :] = source[
                    rows(i, nx - 1 if sign == 1 else 0), :
                ]
                slot += 1
            for extra in extras:
                sx[e, k, slot * ny : (slot + 1) * ny, :] = extra(
                    0, sign, nx - 1 if sign == 1 else 0
                )
                slot += 1
            slot = 0
            edge = ny - 1 if sign == 1 else 0
            for i in movers(orient, 1, sign) if source is not None else ():
                for x in range(nx):
                    sy[e, k, slot * nx + x : slot * nx + x + 1, :] = source[row(i, x, edge), :]
                slot += 1
            for extra in extras:
                for x in range(nx):
                    sy[e, k, slot * nx + x : slot * nx + x + 1, :] = extra(1, sign, x)[
                        edge : edge + 1, :
                    ]
                slot += 1
        if corners:
            for k, (dx, dy) in enumerate(CORNERS):
                i = corner_mover(orient, dx, dy)
                sc[e, k, 0:1, :] = source[
                    row(i, nx - 1 if dx == 1 else 0, ny - 1 if dy == 1 else 0), :
                ]

        def copy(src, dst, n, dx, dy):
            found[n] = pltpu.make_async_remote_copy(
                src_ref=src, dst_ref=dst, send_sem=send.at[e, n], recv_sem=recv.at[e, n],
                device_id=device(dx, dy), device_id_type=MESH,
            )
            found[n].start()

        for k, sign in enumerate(SIGNS):
            copy(sx.at[e, k], rx.at[e, k], k, sign, 0)
            copy(sy.at[e, k], ry.at[e, k], 2 + k, 0, sign)
        if corners:
            for k, (dx, dy) in enumerate(CORNERS):
                copy(sc.at[e, k], rc.at[e, k], 4 + k, dx, dy)
        started.extend(found.values())
        return list(found.values())

    def arrive(copies):
        for c in copies:
            c.wait_recv()

    def moved_x(inside, e, slot, x, sign):
        if 0 <= x - sign < nx:
            return inside(x - sign)
        return rx[e, SIGNS.index(sign), slot * ny : (slot + 1) * ny, :]

    def moved_y(plane, edge_row, sign):
        shifted = pltpu.roll(plane, 1 if sign == 1 else ny - 1, 0)
        edge = 0 if sign == 1 else ny - 1
        return jnp.where(height == edge, jnp.broadcast_to(edge_row, shifted.shape), shifted)

    def moved_z(plane, fill, sign):
        shifted = pltpu.roll(plane, 1 if sign == 1 else nz - 1, 1)
        return jnp.where(depth == (0 if sign == 1 else nz - 1), fill, shifted)

    def face_y(e, slot, x, sign):
        at = slot * nx + x
        return ry[e, SIGNS.index(sign), at : at + 1, :]

    def stream(source, e, orient, store):
        for i, (px, py, pz) in enumerate(steps_of(orient)):
            for x in range(nx):
                plane = None
                if px:
                    plane = moved_x(
                        lambda k: source[rows(i, k), :],
                        e, movers(orient, 0, px).index(i), x, px,
                    )
                else:
                    plane = source[rows(i, x), :]
                if py:
                    if 0 <= x - px < nx:
                        edge = face_y(e, movers(orient, 1, py).index(i), x - px, py)
                    else:
                        edge = rc[e, CORNERS.index((px, py)), 0:1, :]
                    plane = moved_y(plane, edge, py)
                if pz:
                    plane = moved_z(plane, source[rows(OPPOSITE[i], x), :], pz)
                store(i, x, plane)

    def motion(fields, x):
        result = []
        for a in range(3):
            value = None
            for i in range(Q):
                if VELOCITIES[i, a] == 0:
                    continue
                term = fields[rows(i, x), :]
                if value is None:
                    value = term if VELOCITIES[i, a] == 1 else -term
                elif VELOCITIES[i, a] == 1:
                    value = value + term
                else:
                    value = value - term
            result.append(value)
        return result

    def heat_near(field, e, slot, x, a, s):
        if a == 0:
            return moved_x(lambda k: field[k], e, slot, x, -s)
        if a == 1:
            return moved_y(field[x], face_y(e, slot, x, -s), -s)
        return moved_z(field[x], COLD_WALL if s == 1 else HOT_WALL, -s)

    def fluid(x):
        return site[x] == 0

    def liquid(tadj, x):
        return jnp.where(fluid(x), tadj[x], 0.0)

    def flux(speeds, tadj, x, a, s):
        return (CONDUCTIVITY - 0.5 * s * speeds[x][a]) * liquid(tadj, x)

    loads[6].wait()
    to_rows(f0, ft.at[0])
    for first, at in chunks(ny):
        if first == nx // 2 * ny:
            loads[9].wait()
            pl.semaphore_wait(barrier, len(partners))
            copies_0 = begin(1, adj2, -1, [], True)
        pair = hidden(0, at)
        both = dot(m3[...], pair, NN)
        to_planes(both[:ROWS] + both[ROWS:] + col[:ROWS, 1:2], first, net)
    for c in loads[7:9] + loads[10:]:
        c.wait()
    for x in range(nx):
        open_cell = fluid(x)
        for i in range(Q):
            value = f0[rows(i, x), :] + net[rows(i, x), :]
            if BUOYANCY[i] != 0.0:
                value = value + BUOYANCY[i] * t0[x]
            post[rows(i, x), :] = jnp.where(open_cell, value, f0[rows(OPPOSITE[i], x), :])
    copies_a = begin(0, post, 1, [lambda a, s, x: t0[x]], True)

    def incoming(s, adjoint, e_adj):
        lifts = [jnp.zeros((ny, nz), F32) for _ in range(nx)]

        def keep(i, x, plane):
            pcg[rows(i, x), :] = plane
            value = jnp.where(fluid(x), plane, 0.0)
            pcgf[rows(i, x), :] = value
            if BUOYANCY[i] != 0.0:
                lifts[x] = lifts[x] + BUOYANCY[i] * value

        stream(adjoint, e_adj, -1, keep)
        to_rows(pcgf, pt.at[s])
        for first, at in chunks():
            a, b = halves(pt[s, :, at])
            back[:, at] = dot(r3[...], jnp.concatenate([a, b, a], axis=0), NN)
        return lifts

    speeds0 = [motion(f0, x) for x in range(nx)]
    arrive(copies_0)
    lifts = incoming(1, adj2, 1)
    arrive(copies_a)

    def keep_f1(i, x, plane):
        f1[rows(i, x), :] = plane

    stream(post, 0, 1, keep_f1)
    for x in range(nx):
        value = (1.0 - 6.0 * CONDUCTIVITY) * t0[x]
        for a in range(3):
            for s in SIGNS:
                value = value + (CONDUCTIVITY - 0.5 * s * speeds0[x][a]) * heat_near(
                    t0, 0, 5, x, a, s
                )
        t1[x] = jnp.where(fluid(x), value, jnp.where(site[x] == 1, t0[x], HEATER))
    speeds1 = [motion(f1, x) for x in range(nx)]
    copies_b = begin(
        2, None, 1,
        [lambda a, s, x: t1[x], lambda a, s, x: flux(speeds1, tadj2, x, a, s)], False,
    )

    to_rows(f1, ft.at[1])
    for first, at in chunks():
        hidden(1, at)
        network_back(1, at)

    def assemble(speeds, field, tadj, e_heat, heat_slot, e_flux, flux_slot, lifts, new_adj,
                 new_tadj):
        for x in range(nx):
            wet = liquid(tadj, x)
            speed = speeds[x]
            value = (1.0 - 6.0 * CONDUCTIVITY) * wet + jnp.where(site[x] == 1, tadj[x], 0.0)
            for a in range(3):
                for sign in SIGNS:
                    if a == 0:
                        value = value + moved_x(
                            lambda k: flux(speeds, tadj, k, 0, sign), e_flux, flux_slot, x, sign
                        )
                        continue
                    here = (CONDUCTIVITY - 0.5 * sign * speed[a]) * wet
                    if a == 1:
                        value = value + moved_y(here, face_y(e_flux, flux_slot, x, sign), sign)
                    else:
                        value = value + moved_z(here, 0.0, sign)
            new_tadj[x] = value + lifts[x]
            pulls = [
                wet * (0.5 * (heat_near(field, e_heat, heat_slot, x, a, -1)
                              - heat_near(field, e_heat, heat_slot, x, a, 1)))
                for a in range(3)
            ]
            open_cell = fluid(x)
            for i in range(Q):
                value = net[rows(i, x), :] + jnp.where(
                    open_cell, pcg[rows(i, x), :], pcg[rows(OPPOSITE[i], x), :]
                )
                for a in range(3):
                    if VELOCITIES[i, a] == 1:
                        value = value + pulls[a]
                    elif VELOCITIES[i, a] == -1:
                        value = value - pulls[a]
                new_adj[rows(i, x), :] = value

    network_in(1)
    arrive(copies_b)
    assemble(speeds1, t1, tadj2, 2, 0, 2, 1, lifts, adj1, tadj1)
    copies_c = begin(3, adj1, -1, [lambda a, s, x: flux(speeds0, tadj1, x, a, s)], True)
    weight_grads(1)
    arrive(copies_c)
    lifts = incoming(0, adj1, 3)
    for first, at in chunks():
        network_back(0, at)
    results = [
        (adj_out, adj_to), (tadj_out, tadj_to), (gw1, gw1_to), (gb1, gb1_to),
        (gw2, gw2_to), (gb2, gb2_to), (gw3, gw3_to), (gb3, gb3_to),
    ]
    stores = [
        pltpu.make_async_copy(src, dst, stored.at[k]) for k, (src, dst) in enumerate(results)
    ]
    weight_grads(0)

    part = grads.shape[0] // (duo * ngy)

    def block(where):
        index = (where[0] - (gx - spot)) * ngy + where[1]
        return pl.ds(pl.multiple_of(index * part, 8), part)

    def share(src, dst, n, target):
        c = pltpu.make_async_remote_copy(
            src_ref=src, dst_ref=dst, send_sem=gsend.at[n], recv_sem=grecv.at[n],
            device_id=target, device_id_type=MESH,
        )
        c.start()
        started.append(c)
        return c

    mine = block((gx, gy))
    copies = []
    for n, (dx, dy) in enumerate(inner):
        copies.append(share(grads.at[block(near(dx, dy))], parts_y.at[n], n, near(dx, dy)))
    network_in(0)
    assemble(speeds0, t0, tadj1, 0, 5, 3, 5, lifts, adj_out, tadj_out)
    for c in stores[:2]:
        c.start()
    value = grads[mine, :]
    for n, c in enumerate(copies):
        c.wait_recv()
        value = value + parts_y[n]
    parts_x[0] = value
    copies = []
    for d in range(1, outer):
        copies.append(
            share(parts_x.at[0], parts_x.at[d], len(inner) + d - 1, device(duo * d, 0))
        )
    arrive(copies)
    value = None
    for k in range(outer):
        term = parts_x[lax.rem((gx - spot) // duo - k + outer, outer)]
        value = term if value is None else value + term
    total[mine, :] = value
    copies = []
    for n, (dx, dy) in enumerate(inner):
        copies.append(
            share(total.at[mine], total.at[mine], len(inner) + outer - 1 + n, near(dx, dy))
        )
    arrive(copies)
    gw1[...] = total[0:Q, :]
    gb1[...] = total[Q : Q + 1, :]
    gw2[...] = total[at2 : at2 + hid, :]
    gw3[...] = total[at3 : at3 + Q, :]
    gb2[...] = total[at4 : at4 + 1, :]
    gb3[...] = total[at4 + 1 : at4 + 2, 0:Q]
    for c in stores[2:]:
        c.start()
    for c in started:
        c.wait_send()
    for c in stores:
        c.wait()


def hand_out(*refs):
    load, store = refs[-2:]
    n = (len(refs) - 2) // 3
    ins, outs, held = refs[:n], refs[n : 2 * n], refs[2 * n : 3 * n]
    loads = [pltpu.make_async_copy(ins[k], held[k], load.at[k]) for k in range(n)]
    stores = [pltpu.make_async_copy(held[k], outs[k], store.at[k]) for k in range(n)]
    for c in loads:
        c.start()
    for k in range(n):
        loads[k].wait()
        stores[k].start()
    for c in stores:
        c.wait()


def per_device(ngx, ngy, f0, t0, site, w1, b1, w2, b2, w3, b3, adj2, tadj2):
    q, nx, ny, nz = f0.shape
    hid = w2.shape[0]
    sites = nx * ny * nz
    flat = (q * nx * ny, nz)
    factor = 1.0 / math.sqrt(nx * ngx * ny * ngy * nz)
    group = (2 if ngx % 2 == 0 else 1) * ngy
    outer = ngx * ngy // group
    needed = 24 + hid + 24
    unit = 8 * group
    length = -(-needed // unit) * unit
    side = -(-(SLOTS * nx) // 8) * 8
    plane = pltpu.VMEM((nx, ny, nz), F32)
    wide = pltpu.VMEM(flat, F32)
    dma = pltpu.SemaphoreType.DMA
    gcount = 2 * (group - 1) + outer - 1
    scratch = [
        wide, plane, pltpu.VMEM(w1.shape, F32), pltpu.VMEM((1, hid), F32),
        pltpu.VMEM(w2.shape, F32), pltpu.VMEM((1, hid), F32),
        pltpu.VMEM((q, hid), F32), pltpu.VMEM((1, q), F32), dma((8,)),
        wide, plane, pltpu.VMEM((nx, ny, nz), jnp.int32),
        pltpu.VMEM(w1.shape, F32), pltpu.VMEM((1, hid), F32),
        pltpu.VMEM(w2.shape, F32), pltpu.VMEM((1, hid), F32),
        pltpu.VMEM((q, hid), F32), pltpu.VMEM((1, q), F32),
        wide, plane, dma((11,)),
        wide, wide, plane, wide, plane, wide, wide, wide,
        pltpu.VMEM((2, ROWS, sites), F32),
        pltpu.VMEM((2, ROWS, sites), F32),
        pltpu.VMEM((hid, sites), F32),
        pltpu.VMEM((2, hid, sites), F32),
        pltpu.VMEM((2, hid, sites), F32),
        pltpu.VMEM((2, 2 * hid + 16, sites), BF16),
        pltpu.VMEM((2, 2 * hid, sites), BF16),
        pltpu.VMEM((2, 2 * hid, sites), BF16),
        pltpu.VMEM((2, 2 * hid, sites), BF16),
        pltpu.VMEM((hid, hid), F32),
        pltpu.VMEM((hid, 3 * ROWS), BF16),
        pltpu.VMEM((2 * hid, 2 * hid), BF16),
        pltpu.VMEM((2 * ROWS, 2 * hid), BF16),
        pltpu.VMEM((2 * ROWS, 2 * hid), BF16),
        pltpu.VMEM((2 * hid, 2 * hid), BF16),
        pltpu.VMEM((hid, 3 * ROWS), BF16),
        pltpu.VMEM((hid, hid), F32),
        pltpu.VMEM((4, 2, SLOTS * ny, nz), F32),
        pltpu.VMEM((4, 2, side, nz), F32),
        pltpu.VMEM((4, 4, 8, nz), F32),
        pltpu.VMEM((4, 2, SLOTS * ny, nz), F32),
        pltpu.VMEM((4, 2, side, nz), F32),
        pltpu.VMEM((4, 4, 8, nz), F32),
        dma((4, 8)),
        dma((4, 8)),
        pltpu.VMEM((length, LANES), F32),
        pltpu.VMEM((group - 1, length // group, LANES), F32),
        pltpu.VMEM((outer, length // group, LANES), F32),
        pltpu.VMEM((length, LANES), F32),
        dma((gcount,)),
        dma((gcount,)),
    ]
    shape = jax.ShapeDtypeStruct
    anywhere = pl.BlockSpec(memory_space=pltpu.HBM)
    shapes = [
        shape(flat, F32), shape((nx, ny, nz), F32),
        shape(w1.shape, F32), shape((1, hid), F32),
        shape(w2.shape, F32), shape((1, hid), F32),
        shape((q, hid), F32), shape((1, q), F32),
    ]
    outs = pl.pallas_call(
        functools.partial(kernel, (nx, ny, nz, ngx, ngy, factor)),
        out_shape=shapes,
        in_specs=[anywhere] * 11,
        out_specs=[anywhere] * 8,
        scratch_shapes=scratch,
        compiler_params=pltpu.CompilerParams(
            collective_id=0, has_side_effects=True, vmem_limit_bytes=64 * 1024 * 1024
        ),
    )(
        f0.reshape(flat), t0, site, w1, b1.reshape(1, hid), w2, b2.reshape(1, hid),
        w3.T, b3.reshape(1, q), adj2.reshape(flat), tadj2,
    )
    outs = pl.pallas_call(
        hand_out,
        out_shape=shapes,
        in_specs=[anywhere] * 8,
        out_specs=[anywhere] * 8,
        scratch_shapes=[pltpu.VMEM(s.shape, s.dtype) for s in shapes] + [dma((8,)), dma((8,))],
        compiler_params=pltpu.CompilerParams(vmem_limit_bytes=64 * 1024 * 1024),
    )(*outs)
    return (
        outs[0].reshape(f0.shape), outs[1], outs[2], outs[3].reshape(hid),
        outs[4], outs[5].reshape(hid), outs[6].T, outs[7].reshape(q),
    )


def solution(mesh):
    grid = P(None, "gx", "gy", None)
    plane = P("gx", "gy", None)
    in_specs = (grid, plane, plane) + (P(),) * 6 + (grid, plane)
    out_specs = (grid, plane) + (P(),) * 6
    return jax.shard_map(
        functools.partial(per_device, mesh.shape["gx"], mesh.shape["gy"]),
        mesh=mesh, in_specs=in_specs, out_specs=out_specs, check_vma=False,
    )
```
